512 devices in a mesh: group: 16 (over z_lo, x, core), expert: 32 (over y, z_hi).
Axes of the slice: x: 4, y: 8, z: 8 (z_hi: 4, z_lo: 2; z = z_hi * 2 + z_lo), core: 2. Of those that a mesh axis runs over, the one named last changes fastest.
Arguments:
- hidden: bfloat16 [3, 16384, 1024], P(None, ('group', 'expert')), may hold values from -6 to 6
- norm_gain: float32 [1024], replicated, may hold values from 0.1 to 1.9
- routes: int32 [3, 16384, 8], P(None, ('group', 'expert')), may hold values from 0 to 63, all different within a row; in each aligned block of 32 rows (0 to 31, 32 to 63, ..., all dimensions but the last counted through in order) at most 8 rows name the same one
- gates: float32 [3, 16384, 8], P(None, ('group', 'expert')), may hold values from 0.1 to 1
- switch: int32 [64], replicated, may hold values from 0 to 3
- experts_old: bfloat16 [64, 3, 384, 1024], P('expert', None, 'group'), may hold values from -0.25 to 0.25
- experts_new: bfloat16 [64, 3, 384, 1024], P('expert', None, 'group'), may hold values from -0.25 to 0.25
Outputs:
- mixed: bfloat16 [3, 16384, 1024], P(None, ('group', 'expert'))
The draws below stay inside these ranges and needn't reach their ends.
Inputs may be any that keep to these rules, and one draw needn't show every extreme that they name: `routes`: in each step, no expert is named by more than 8 of one device's rows (aligned blocks of 32 rows); some expert is named by exactly 8 of them. A row names 8 different experts. `switch`: A value of 0 means the expert uses its new weights in every step; a value of 3 means it never does.
All inputs are finite; a program needn't handle non-finite values.
Results may differ from the reference program's by a relative error of at most 0.0065.
Values may be sent and summed in bfloat16 or wider, within the bound.
No kernel may reach another device: no remote copies, remote signals or barrier semaphores. Data moves between devices by JAX's collectives and lax.ppermute only.
A program may use at most 64 MiB of HBM per device.

```python
import math
import jax
import jax.numpy as jnp
import numpy as np
from jax import lax

D = 1024
FF = 384
TOP = 8
STEPS = 3
ROW_DEV = 32
EXPERTS = 64
CAP = 8
ROWS = 16384
N_GROUP = 16
N_EXPERT = 32


def with_ends(entries, rng, smallest, high):
    index_at = [jax.random.randint(jax.random.fold_in(rng, axis), (), 0, length) for axis, length in enumerate(entries.shape)]
    longest = entries.shape.index(max(entries.shape))
    neighbour = index_at[:longest] + [(index_at[longest] + 1) % entries.shape[longest]] + index_at[longest + 1:]
    return entries.at[tuple(index_at)].set(smallest).at[tuple(neighbour)].set(high)


def steps_of(key, extent, split, smallest, top_value):
    gain = 1.0
    for dim, blocks in split:
        heights = jax.random.uniform(jax.random.fold_in(jax.random.fold_in(key, 6), dim), (blocks,), jnp.float32, smallest / len(split), top_value / len(split))
        gain = gain * jnp.repeat(jnp.exp(heights), extent[dim] // blocks).reshape((-1,) + (1,) * (len(extent) - 1 - dim))
    return gain


def routed_block(stream_key, own, number, rows, amount, top, limit, lean):
    ranking = jax.random.permutation(stream_key, amount)
    heavy_load, common = shares(amount, rows * top, limit, lean, True), shares(amount, rows * top, limit, lean, False)
    places = jnp.arange(amount)

    def named(sizes, offset_by):
        used = int((sizes > 0).sum())
        fixed = max(1, used // 4)
        moved = fixed + (places - fixed + offset_by * (used - fixed)) % max(1, amount - fixed)
        return jnp.zeros((amount,), jnp.int32).at[ranking[jnp.where(places < fixed, places, moved)]].set(jnp.asarray(sizes, jnp.int32))

    sizes = jnp.where(number % 4 == 0, named(heavy_load, number // 4), named(common, number - number // 4 - 1))
    mixed = jax.random.permutation(jax.random.fold_in(own, 3), amount)
    source_of, receiver = mixed[0:amount // 2 * 2:2], mixed[1:amount // 2 * 2:2]
    margin = jnp.minimum(sizes[source_of] - 1, limit - sizes[receiver]) // 2
    margin = jnp.where((source_of == ranking[0]) | (receiver == ranking[0]) | (sizes[receiver] == 0), 0, jnp.maximum(margin, 0))
    moved = jax.random.randint(jax.random.fold_in(own, 4), (amount // 2,), 0, 1 << 20) % (margin + 1)
    sizes = sizes.at[source_of].add(-moved).at[receiver].add(moved)
    items = jnp.searchsorted(jnp.cumsum(sizes), jnp.arange(rows * top), side="right").astype(jnp.int32)
    grid = items.reshape(top, rows).T
    grid = grid[jax.random.permutation(jax.random.fold_in(own, 1), rows)]
    offset_by = jax.random.randint(jax.random.fold_in(own, 2), (rows, 1), 0, top)
    return jnp.take_along_axis(grid, (jnp.arange(top)[None, :] + offset_by) % top, axis=1)


def shares(amount, total, bound, skew, full):
    loads = [(1 << 20) // math.isqrt(standing ** skew) + 1 for standing in range(1, amount + 1)]
    largest = bound if full else min(bound, max(-(-total // amount), total * loads[0] // sum(loads)))
    least = 1 if total - largest >= amount - 1 else 0
    holding, surplus = [largest] + [least] * (amount - 1), total - largest - least * (amount - 1)
    while surplus > 0:
        movable = [i for i in range(1, amount) if holding[i] < largest] or [i for i in range(1, amount) if holding[i] < bound]
        whole, left = sum([loads[i] for i in movable]), surplus
        for i in movable:
            extra = min(bound - holding[i], max(1, left * loads[i] // whole), surplus)
            holding[i] = holding[i] + extra
            surplus = surplus - extra
    return np.array(holding)


def gaussian(own_key, shape, spread, bound, pieces=(), held_as=jnp.bfloat16):
    factor_of = steps_of(own_key, shape, pieces, -0.22, 0.18) if pieces else 1.0
    result = jax.random.normal(own_key, shape, jnp.float32) * spread * factor_of
    return jnp.minimum(jnp.maximum(result, -bound), bound).astype(held_as)


def setup_inputs(seed: int = 0) -> dict:
    keys = jax.random.split(jax.random.key(seed), 8)
    hidden = gaussian(keys[0], (STEPS, ROWS, D), 1.0, 6.0, ((1, 512),))
    norm_gain = jnp.clip(1.0 + 0.18 * jax.random.normal(keys[1], (D,), jnp.float32), 0.1, 1.9)
    routes_keys = jax.random.split(jax.random.fold_in(keys[2], 1), STEPS * ROWS // ROW_DEV)
    routes_turns = jax.random.permutation(jax.random.fold_in(keys[2], 3), STEPS * ROWS // ROW_DEV)
    routes = jax.vmap(lambda own, number: routed_block(jax.random.fold_in(keys[2], 2), own, number, ROW_DEV, EXPERTS, TOP, CAP, 2))(routes_keys, routes_turns).reshape((STEPS, ROWS, TOP))
    gates = jnp.clip(jnp.exp(math.log(1.0) - 2.3025851 * jax.random.uniform(keys[3], (STEPS, ROWS, TOP), jnp.float32) ** steps_of(keys[3], (STEPS, ROWS, TOP), ((1, 512),), -0.2, 0.2)), 0.1, 1.0)
    switch = with_ends(jax.random.randint(keys[4], (EXPERTS,), 0, STEPS + 1), jax.random.fold_in(keys[4], 1), 0, STEPS).astype(jnp.int32)
    experts_old = gaussian(keys[5], (EXPERTS, 3, FF, D), ((D * FF) ** 0.5) ** -0.5, 0.25, ((0, 32), (2, 16)))
    experts_new = gaussian(keys[6], (EXPERTS, 3, FF, D), ((D * FF) ** 0.5) ** -0.5, 0.25, ((0, 32), (2, 16)))
    return dict(hidden=hidden, norm_gain=norm_gain, routes=routes, gates=gates, switch=switch, experts_old=experts_old, experts_new=experts_new)


def expert_out(rows_in, weights):
    gate_v = jnp.dot(rows_in, weights[0].T, preferred_element_type=jnp.float32)
    up_v = jnp.dot(rows_in, weights[1].T, preferred_element_type=jnp.float32)
    act = (jax.nn.silu(gate_v) * up_v).astype(jnp.bfloat16)
    return jnp.dot(act, weights[2], preferred_element_type=jnp.float32).astype(jnp.bfloat16)

def reference(hidden, norm_gain, routes, gates, switch, experts_old, experts_new):
    xf = hidden.astype(jnp.float32)
    scale = lax.rsqrt(lax.optimization_barrier(jnp.mean(xf * xf, axis=-1, keepdims=True)) + 1e-06)
    normed = (xf * scale * norm_gain).astype(jnp.bfloat16)
    load = N_GROUP * N_EXPERT * CAP
    results = []
    for step in range(STEPS):
        step_routes = routes[step]
        step_gates = gates[step]
        step_rows = normed[step]

        def one(carry, index):
            use_new = step >= switch[index]
            weights = jnp.where(use_new, experts_new[index], experts_old[index])
            hit = step_routes == index
            weight = lax.optimization_barrier(jnp.sum(jnp.where(hit, step_gates, 0.0), axis=1))
            picked = jnp.any(hit, axis=1)
            places = jnp.nonzero(picked, size=load, fill_value=0)[0].astype(jnp.int32)
            valid = jnp.arange(load) < jnp.sum(picked.astype(jnp.int32))
            outputs = expert_out(step_rows[places], weights).astype(jnp.float32)
            factor = jnp.where(valid, weight[places], 0.0)
            return (carry.at[places].add(factor[:, None] * outputs), None)
        start = jnp.zeros((ROWS, D), jnp.float32)
        total, _ = lax.scan(one, start, jnp.arange(EXPERTS, dtype=jnp.int32))
        results.append((xf[step] + total).astype(jnp.bfloat16))
    return jnp.stack(results)
```

```python
import jax
import jax.numpy as jnp
from jax import lax
from jax.experimental import pallas as pl
from jax.experimental.pallas import tpu as pltpu
from jax.sharding import PartitionSpec as P

CAP = 8
F32 = jnp.float32
BF16 = jnp.bfloat16


def slot_mask(routes, experts):
    rows, top = routes.shape
    slots = experts * CAP
    lane = lax.broadcasted_iota(jnp.int32, (rows, slots), 1)
    owner = lane >> 3
    named = routes[:, 0:1] == owner
    for k in range(1, top):
        named = named | (routes[:, k : k + 1] == owner)
    earlier = lax.broadcasted_iota(jnp.int32, (rows, rows), 1) < lax.broadcasted_iota(
        jnp.int32, (rows, rows), 0
    )
    rank = jnp.dot(
        earlier.astype(F32).astype(BF16), named.astype(F32).astype(BF16), preferred_element_type=F32
    )
    return named & (rank == (lane & 7).astype(F32))


def pack_kernel(hidden_ref, gain_ref, routes_ref, out_ref):
    steps, rows, width = hidden_ref.shape
    members, _, per, _ = out_ref.shape
    for step in range(steps):
        xf = hidden_ref[step].astype(F32)
        scale = lax.rsqrt(jnp.mean(xf * xf, axis=-1, keepdims=True) + 1e-06)
        normed = (xf * scale * gain_ref[...]).astype(BF16)
        spread = slot_mask(routes_ref[step], members * per // CAP).astype(F32).astype(BF16)
        packed = lax.dot_general(
            spread, normed, (((0,), (0,)), ((), ())), preferred_element_type=F32
        )
        out_ref[:, step] = packed.astype(BF16).reshape(members, per, width)


def weigh_kernel(routes_ref, gates_ref, out_ref):
    steps, rows, top = routes_ref.shape
    slots = out_ref.shape[2]
    for step in range(steps):
        routes = routes_ref[step]
        gates = gates_ref[step]
        mask = slot_mask(routes, slots // CAP)
        owner = lax.broadcasted_iota(jnp.int32, (rows, slots), 1) >> 3
        weight = jnp.zeros((rows, slots), F32)
        for k in range(top):
            weight = jnp.where(routes[:, k : k + 1] == owner, gates[:, k : k + 1], weight)
        weight = jnp.where(mask, weight, 0.0)
        high = weight.astype(BF16)
        rest = weight - high.astype(F32)
        mid = rest.astype(BF16)
        low = (rest - mid.astype(F32)).astype(BF16)
        out_ref[step, 0:rows] = high
        out_ref[step, rows : 2 * rows] = mid
        out_ref[step, 2 * rows : 3 * rows] = low


def expert_kernel(version_ref, rows_ref, weights_ref, out_ref, held_ref):
    members, _, per, width = rows_ref.shape
    e = pl.program_id(1)
    both = rows_ref[:, 0].astype(F32)
    nt = (((1,), (1,)), ((), ()))

    def expert(mine):
        rows_in = mine.reshape(members * CAP, width).astype(BF16)
        gate_v = lax.dot_general(rows_in, weights_ref[0, 0, 0], nt, preferred_element_type=F32)
        up_v = lax.dot_general(rows_in, weights_ref[0, 0, 1], nt, preferred_element_type=F32)
        act = (gate_v / (1.0 + jnp.exp(-gate_v)) * up_v).astype(BF16)
        made = jnp.dot(act, weights_ref[0, 0, 2], preferred_element_type=F32)
        return made.reshape(members, CAP, width)

    @pl.when(e == 0)
    def _():
        held_ref[...] = expert(both[:, :CAP])

    @pl.when(e == 1)
    def _():
        made = expert(both[:, CAP:])
        out_ref[:, 0] = jnp.concatenate([held_ref[...], made], axis=1).astype(BF16)


def combine_kernel(hidden_ref, weights_ref, back_ref, out_ref):
    steps, rows, width = hidden_ref.shape
    members, _, per, _ = back_ref.shape
    for step in range(steps):
        outputs = back_ref[:, step].reshape(members * per, width)
        parts = jnp.dot(weights_ref[step], outputs, preferred_element_type=F32)
        total = parts[2 * rows :] + parts[rows : 2 * rows] + parts[:rows]
        out_ref[step] = (hidden_ref[step].astype(F32) + total).astype(BF16)


def local(hidden, norm_gain, routes, gates, switch, experts_old, experts_new):
    steps, rows, width = hidden.shape
    exp_dev, mats, shard, _ = experts_old.shape
    members = lax.axis_size("expert")
    groups = lax.axis_size("group")
    per = exp_dev * CAP
    slots = members * per
    big = pltpu.CompilerParams(vmem_limit_bytes=48 * 1024 * 1024)

    both = jnp.stack([experts_old, experts_new])
    weights = lax.all_gather(both, "group", axis=3, tiled=True)

    outgoing = pl.pallas_call(
        pack_kernel,
        out_shape=jax.ShapeDtypeStruct((members, steps, per, width), BF16),
        compiler_params=big,
        name="pack",
    )(hidden, norm_gain.reshape(1, width), routes)
    received = lax.all_to_all(outgoing, "expert", split_axis=0, concat_axis=0, tiled=True)
    weigh = pl.pallas_call(
        weigh_kernel,
        out_shape=jax.ShapeDtypeStruct((steps, 3 * rows, slots), BF16),
        compiler_params=big,
        name="weigh",
    )(routes, gates)

    mine = lax.dynamic_slice_in_dim(switch, lax.axis_index("expert") * exp_dev, exp_dev, 0)
    version = (jnp.arange(steps, dtype=jnp.int32)[:, None] >= mine).astype(jnp.int32).reshape(-1)
    produced = pl.pallas_call(
        expert_kernel,
        grid_spec=pltpu.PrefetchScalarGridSpec(
            num_scalar_prefetch=1,
            grid=(steps, exp_dev),
            in_specs=[
                pl.BlockSpec((members, 1, per, width), lambda s, e, v: (0, s, 0, 0)),
                pl.BlockSpec(
                    (1, 1, mats, shard * groups, width), lambda s, e, v: (v[s * 2 + e], e, 0, 0, 0)
                ),
            ],
            out_specs=pl.BlockSpec((members, 1, per, width), lambda s, e, v: (0, s, 0, 0)),
            scratch_shapes=[pltpu.VMEM((members, CAP, width), F32)],
        ),
        out_shape=jax.ShapeDtypeStruct((members, steps, per, width), BF16),
        compiler_params=big,
        name="experts",
    )(version, received, weights)
    returned = lax.all_to_all(produced, "expert", split_axis=0, concat_axis=0, tiled=True)
    return pl.pallas_call(
        combine_kernel,
        out_shape=jax.ShapeDtypeStruct((steps, rows, width), BF16),
        compiler_params=big,
        name="combine",
    )(hidden, weigh, returned)


def solution(mesh):
    in_specs = (
        P(None, ("group", "expert"), None),
        P(),
        P(None, ("group", "expert"), None),
        P(None, ("group", "expert"), None),
        P(),
        P("expert", None, "group", None),
        P("expert", None, "group", None),
    )
    out_specs = P(None, ("group", "expert"), None)
    return jax.shard_map(local, mesh=mesh, in_specs=in_specs, out_specs=out_specs, check_vma=False)
```

```python
import jax
import jax.numpy as jnp
from jax import lax
from jax.experimental import pallas as pl
from jax.experimental.pallas import tpu as pltpu
from jax.sharding import PartitionSpec as P

CAP = 8
F32 = jnp.float32
BF16 = jnp.bfloat16


def slot_mask(routes, experts):
    rows, top = routes.shape
    slots = experts * CAP
    lane = lax.broadcasted_iota(jnp.int32, (rows, slots), 1)
    owner = lane >> 3
    named = routes[:, 0:1] == owner
    for k in range(1, top):
        named = named | (routes[:, k : k + 1] == owner)
    earlier = lax.broadcasted_iota(jnp.int32, (rows, rows), 1) < lax.broadcasted_iota(
        jnp.int32, (rows, rows), 0
    )
    rank = jnp.dot(
        earlier.astype(F32).astype(BF16), named.astype(F32).astype(BF16), preferred_element_type=F32
    )
    return named & (rank == (lane & 7).astype(F32))


def pack_kernel(hidden_ref, gain_ref, routes_ref, gates_ref, out_ref, weights_ref):
    steps, rows, width = hidden_ref.shape
    members, _, per, _ = out_ref.shape
    slots = members * per
    owner = lax.broadcasted_iota(jnp.int32, (rows, slots), 1) >> 3
    for step in range(steps):
        xf = hidden_ref[step].astype(F32)
        scale = lax.rsqrt(jnp.mean(xf * xf, axis=-1, keepdims=True) + 1e-06)
        normed = (xf * scale * gain_ref[...]).astype(BF16)
        routes = routes_ref[step]
        gates = gates_ref[step]
        mask = slot_mask(routes, slots // CAP)
        spread = mask.astype(F32).astype(BF16)
        packed = lax.dot_general(
            spread, normed, (((0,), (0,)), ((), ())), preferred_element_type=F32
        )
        out_ref[:, step] = packed.astype(BF16).reshape(members, per, width)
        weight = jnp.zeros((rows, slots), F32)
        for k in range(routes.shape[1]):
            weight = jnp.where(routes[:, k : k + 1] == owner, gates[:, k : k + 1], weight)
        weight = jnp.where(mask, weight, 0.0)
        high = weight.astype(BF16)
        rest = weight - high.astype(F32)
        mid = rest.astype(BF16)
        low = (rest - mid.astype(F32)).astype(BF16)
        weights_ref[step, 0:rows] = high
        weights_ref[step, rows : 2 * rows] = mid
        weights_ref[step, 2 * rows : 3 * rows] = low


def expert_kernel(version_ref, rows_ref, weights_ref, out_ref, held_ref):
    members, _, per, width = rows_ref.shape
    e = pl.program_id(1)
    both = rows_ref[:, 0].astype(F32)
    nt = (((1,), (1,)), ((), ()))

    def expert(mine):
        rows_in = mine.reshape(members * CAP, width).astype(BF16)
        gate_v = lax.dot_general(rows_in, weights_ref[0, 0, 0], nt, preferred_element_type=F32)
        up_v = lax.dot_general(rows_in, weights_ref[0, 0, 1], nt, preferred_element_type=F32)
        act = (gate_v / (1.0 + jnp.exp(-gate_v)) * up_v).astype(BF16)
        made = jnp.dot(act, weights_ref[0, 0, 2], preferred_element_type=F32)
        return made.reshape(members, CAP, width)

    @pl.when(e == 0)
    def _():
        held_ref[...] = expert(both[:, :CAP])

    @pl.when(e == 1)
    def _():
        made = expert(both[:, CAP:])
        out_ref[:, 0] = jnp.concatenate([held_ref[...], made], axis=1).astype(BF16)


def combine_kernel(hidden_ref, weights_ref, back_ref, out_ref):
    steps, rows, width = hidden_ref.shape
    members, _, per, _ = back_ref.shape
    for step in range(steps):
        outputs = back_ref[:, step].reshape(members * per, width)
        parts = jnp.dot(weights_ref[step], outputs, preferred_element_type=F32)
        total = parts[2 * rows :] + parts[rows : 2 * rows] + parts[:rows]
        out_ref[step] = (hidden_ref[step].astype(F32) + total).astype(BF16)


def local(hidden, norm_gain, routes, gates, switch, experts_old, experts_new):
    steps, rows, width = hidden.shape
    exp_dev, mats, shard, _ = experts_old.shape
    members = lax.axis_size("expert")
    groups = lax.axis_size("group")
    per = exp_dev * CAP
    slots = members * per
    big = pltpu.CompilerParams(vmem_limit_bytes=48 * 1024 * 1024)

    half = groups // 2
    swap = [(i, (i + half) % groups) for i in range(groups)]
    planes = [list(range(half)), list(range(half, groups))]
    others = [lax.ppermute(shard_of, "group", swap) for shard_of in (experts_old, experts_new)]
    outgoing, weigh = pl.pallas_call(
        pack_kernel,
        out_shape=(
            jax.ShapeDtypeStruct((members, steps, per, width), BF16),
            jax.ShapeDtypeStruct((steps, 3 * rows, slots), BF16),
        ),
        compiler_params=big,
        cost_estimate=pl.CostEstimate(
            flops=2 * steps * rows * slots * width, bytes_accessed=4 << 20, transcendentals=0
        ),
        name="pack",
    )(hidden, norm_gain.reshape(1, width), routes, gates)
    others, outgoing = lax.optimization_barrier((others, outgoing))
    shards = [
        jnp.concatenate(pair, axis=2) for pair in zip((experts_old, experts_new), others)
    ]
    weights = lax.all_gather(
        jnp.stack(shards), "group", axis=3, tiled=True, axis_index_groups=planes
    )
    received = lax.all_to_all(outgoing, "expert", split_axis=0, concat_axis=0, tiled=True)

    mine = lax.dynamic_slice_in_dim(switch, lax.axis_index("expert") * exp_dev, exp_dev, 0)
    version = (jnp.arange(steps, dtype=jnp.int32)[:, None] >= mine).astype(jnp.int32).reshape(-1)
    produced = pl.pallas_call(
        expert_kernel,
        grid_spec=pltpu.PrefetchScalarGridSpec(
            num_scalar_prefetch=1,
            grid=(steps, exp_dev),
            in_specs=[
                pl.BlockSpec((members, 1, per, width), lambda s, e, v: (0, s, 0, 0)),
                pl.BlockSpec(
                    (1, 1, mats, shard * groups, width), lambda s, e, v: (v[s * 2 + e], e, 0, 0, 0)
                ),
            ],
            out_specs=pl.BlockSpec((members, 1, per, width), lambda s, e, v: (0, s, 0, 0)),
            scratch_shapes=[pltpu.VMEM((members, CAP, width), F32)],
        ),
        out_shape=jax.ShapeDtypeStruct((members, steps, per, width), BF16),
        compiler_params=big,
        name="experts",
    )(version, received, weights)
    returned = lax.all_to_all(produced, "expert", split_axis=0, concat_axis=0, tiled=True)
    return pl.pallas_call(
        combine_kernel,
        out_shape=jax.ShapeDtypeStruct((steps, rows, width), BF16),
        compiler_params=big,
        name="combine",
    )(hidden, weigh, returned)


def solution(mesh):
    in_specs = (
        P(None, ("group", "expert"), None),
        P(),
        P(None, ("group", "expert"), None),
        P(None, ("group", "expert"), None),
        P(),
        P("expert", None, "group", None),
        P("expert", None, "group", None),
    )
    out_specs = P(None, ("group", "expert"), None)
    return jax.shard_map(local, mesh=mesh, in_specs=in_specs, out_specs=out_specs, check_vma=False)
```

```python
import jax
import jax.numpy as jnp
from jax import lax
from jax.experimental import pallas as pl
from jax.experimental.pallas import tpu as pltpu
from jax.sharding import PartitionSpec as P

CAP = 8
F32 = jnp.float32
BF16 = jnp.bfloat16


def slot_mask(routes, experts):
    rows, top = routes.shape
    slots = experts * CAP
    lane = lax.broadcasted_iota(jnp.int32, (rows, slots), 1)
    owner = lane >> 3
    named = routes[:, 0:1] == owner
    for k in range(1, top):
        named = named | (routes[:, k : k + 1] == owner)
    earlier = lax.broadcasted_iota(jnp.int32, (rows, rows), 1) < lax.broadcasted_iota(
        jnp.int32, (rows, rows), 0
    )
    rank = jnp.dot(
        earlier.astype(F32).astype(BF16), named.astype(F32).astype(BF16), preferred_element_type=F32
    )
    return named & (rank == (lane & 7).astype(F32))


def pack_kernel(
    hidden_hbm, gain_hbm, routes_hbm, gates_hbm, out_ref, weights_ref, hidden, gain, routes, gates, sem
):
    copies = [
        pltpu.make_async_copy(source, held, sem.at[i])
        for i, (source, held) in enumerate(
            ((routes_hbm, routes), (gates_hbm, gates), (hidden_hbm, hidden), (gain_hbm, gain))
        )
    ]
    for copy in copies:
        copy.start()
    for copy in copies:
        copy.wait()
    steps, rows, width = hidden.shape
    experts = out_ref.shape[0]
    slots = experts * CAP
    owner = lax.broadcasted_iota(jnp.int32, (rows, slots), 1) >> 3
    for step in range(steps):
        xf = hidden[step].astype(F32)
        scale = lax.rsqrt(jnp.mean(xf * xf, axis=-1, keepdims=True) + 1e-06)
        normed = (xf * scale * gain[...]).astype(BF16)
        named_by = routes[step].T
        gate_of = gates[step].T
        mask = slot_mask(named_by, experts)
        spread = mask.astype(F32).astype(BF16)
        packed = lax.dot_general(
            spread, normed, (((0,), (0,)), ((), ())), preferred_element_type=F32
        )
        out_ref[:, step] = packed.reshape(experts, CAP, width).astype(BF16)
        weight = jnp.zeros((rows, slots), F32)
        for k in range(named_by.shape[1]):
            weight = jnp.where(named_by[:, k : k + 1] == owner, gate_of[:, k : k + 1], weight)
        weight = jnp.where(mask, weight, 0.0)
        high = weight.astype(BF16)
        rest = weight - high.astype(F32)
        mid = rest.astype(BF16)
        low = (rest - mid.astype(F32)).astype(BF16)
        weights_ref[step, 0:rows] = high
        weights_ref[step, rows : 2 * rows] = mid
        weights_ref[step, 2 * rows : 3 * rows] = low


def expert_kernel(version_ref, rows_ref, *refs):
    weights_refs, out_ref = refs[:-1], refs[-1]
    sources, _, cap, width = rows_ref.shape
    step = pl.program_id(0)
    nt = (((1,), (1,)), ((), ()))

    def matrix(i):
        return jnp.concatenate([ref[0, i] for ref in weights_refs], axis=0)

    rows_in = rows_ref[:, step].astype(F32).reshape(sources * cap, width).astype(BF16)
    gate_v = lax.dot_general(rows_in, matrix(0), nt, preferred_element_type=F32)
    up_v = lax.dot_general(rows_in, matrix(1), nt, preferred_element_type=F32)
    act = (gate_v / (1.0 + jnp.exp(-gate_v)) * up_v).astype(BF16)
    made = jnp.dot(act, matrix(2), preferred_element_type=F32)
    out_ref[:, step] = made.reshape(sources, cap, width).astype(BF16)


def combine_kernel(hidden_ref, weights_ref, back_ref, out_ref):
    steps, rows, width = hidden_ref.shape
    experts, _, cap, _ = back_ref.shape
    for step in range(steps):
        outputs = back_ref[:, step].astype(F32).reshape(experts * cap, width).astype(BF16)
        parts = jnp.dot(weights_ref[step], outputs, preferred_element_type=F32)
        total = parts[2 * rows :] + parts[rows : 2 * rows] + parts[:rows]
        out_ref[step] = (hidden_ref[step].astype(F32) + total).astype(BF16)


def local(hidden, norm_gain, routes, gates, switch, experts_old, experts_new):
    steps, rows, width = hidden.shape
    top = routes.shape[2]
    exp_dev, mats, shard, _ = experts_old.shape
    members = lax.axis_size("expert")
    groups = lax.axis_size("group")
    experts = exp_dev * members
    slots = experts * CAP
    big = pltpu.CompilerParams(vmem_limit_bytes=48 * 1024 * 1024)
    plane = groups // 2
    core = lax.axis_index("group") % 2

    def device(low, x, c):
        return (low % 2) * plane + (x % (plane // 2)) * 2 + c % 2

    def move(array, low, x, c):
        pairs = [
            (device(l, i, k), device(l + low, i + x, k + c))
            for l in range(2)
            for i in range(plane // 2)
            for k in range(2)
        ]
        return lax.ppermute(array, "group", pairs)

    bend = lambda e: (e + 1) % 4 // 2
    rings = [
        [device(low + bend(e), x, c) * members + e for e in range(members) for c in range(2)]
        for low in range(2)
        for x in range(plane // 2)
    ]

    def exchange(blocks):
        return lax.all_to_all(
            blocks, ("group", "expert"), 0, 0, axis_index_groups=rings, tiled=True
        )

    versions = jnp.stack([experts_old, experts_new])
    mine = lax.dynamic_index_in_dim(versions, core, 1, keepdims=False)
    theirs = lax.dynamic_index_in_dim(versions, 1 - core, 1, keepdims=False)
    near = [mine, move(mine, 1, 0, 0), move(theirs, 1, 0, 1), move(theirs, 0, 0, 1)]

    far = lambda array: pltpu.with_memory_space_constraint(array, pltpu.HBM)
    outgoing, weigh = pl.pallas_call(
        pack_kernel,
        in_specs=[pl.BlockSpec(memory_space=pltpu.HBM)] * 4,
        out_shape=(
            jax.ShapeDtypeStruct((experts, steps, CAP, width), BF16),
            jax.ShapeDtypeStruct((steps, 3 * rows, slots), BF16),
        ),
        scratch_shapes=[
            pltpu.VMEM(hidden.shape, BF16),
            pltpu.VMEM((1, width), F32),
            pltpu.VMEM((steps, top, rows), jnp.int32),
            pltpu.VMEM((steps, top, rows), F32),
            pltpu.SemaphoreType.DMA((4,)),
        ],
        compiler_params=big,
        cost_estimate=pl.CostEstimate(
            flops=2 * steps * rows * slots * width, bytes_accessed=4 << 20, transcendentals=0
        ),
        name="pack",
    )(
        far(hidden),
        far(norm_gain.reshape(1, width)),
        far(routes.transpose(0, 2, 1)),
        far(gates.transpose(0, 2, 1)),
    )
    near, outgoing = lax.optimization_barrier((near, outgoing))
    received = exchange(outgoing)
    block = jnp.concatenate(near, axis=2)
    blocks = [block] + [move(block, 0, x, 0) for x in (2, 1, -1)]

    own = lax.axis_index("expert") * exp_dev + core
    version = (jnp.arange(steps, dtype=jnp.int32) >= switch[own]).astype(jnp.int32)
    whole = pl.BlockSpec(memory_space=pltpu.VMEM)
    produced = pl.pallas_call(
        expert_kernel,
        grid_spec=pltpu.PrefetchScalarGridSpec(
            num_scalar_prefetch=1,
            grid=(steps,),
            in_specs=[whole]
            + [pl.BlockSpec((1,) + block.shape[1:], lambda s, v: (v[s], 0, 0, 0))] * len(blocks),
            out_specs=whole,
        ),
        out_shape=jax.ShapeDtypeStruct((experts, steps, CAP, width), BF16),
        compiler_params=big,
        name="experts",
    )(version, received, *blocks)
    returned = exchange(produced)
    return pl.pallas_call(
        combine_kernel,
        out_shape=jax.ShapeDtypeStruct((steps, rows, width), BF16),
        compiler_params=big,
        name="combine",
    )(hidden, weigh, returned)


def solution(mesh):
    in_specs = (
        P(None, ("group", "expert"), None),
        P(),
        P(None, ("group", "expert"), None),
        P(None, ("group", "expert"), None),
        P(),
        P("expert", None, "group", None),
        P("expert", None, "group", None),
    )
    out_specs = P(None, ("group", "expert"), None)
    return jax.shard_map(local, mesh=mesh, in_specs=in_specs, out_specs=out_specs, check_vma=False)
```

```python
import jax
import jax.numpy as jnp
from jax import lax
from jax.experimental import pallas as pl
from jax.experimental.pallas import tpu as pltpu
from jax.sharding import PartitionSpec as P

CAP = 8
F32 = jnp.float32
BF16 = jnp.bfloat16


def slot_mask(routes, experts):
    rows, top = routes.shape
    slots = experts * CAP
    lane = lax.broadcasted_iota(jnp.int32, (rows, slots), 1)
    owner = lane >> 3
    named = routes[:, 0:1] == owner
    for k in range(1, top):
        named = named | (routes[:, k : k + 1] == owner)
    earlier = lax.broadcasted_iota(jnp.int32, (rows, rows), 1) < lax.broadcasted_iota(
        jnp.int32, (rows, rows), 0
    )
    rank = jnp.dot(
        earlier.astype(F32).astype(BF16), named.astype(F32).astype(BF16), preferred_element_type=F32
    )
    return named & (rank == (lane & 7).astype(F32))


def pack_kernel(
    hidden_hbm, gain_hbm, routes_hbm, out_hbm, hidden, gain, routes, packed, in_sem, out_sem
):
    copies = [
        pltpu.make_async_copy(source, held, in_sem.at[i])
        for i, (source, held) in enumerate(
            ((routes_hbm, routes), (hidden_hbm, hidden), (gain_hbm, gain))
        )
    ]
    for copy in copies:
        copy.start()
    for copy in copies:
        copy.wait()
    steps, experts, cap, width = packed.shape
    leaving = []
    for step in range(steps):
        xf = hidden[step].astype(F32)
        scale = lax.rsqrt(jnp.mean(xf * xf, axis=-1, keepdims=True) + 1e-06)
        normed = (xf * scale * gain[...]).astype(BF16)
        spread = slot_mask(routes[step].T, experts).astype(F32).astype(BF16)
        rows_out = lax.dot_general(
            spread, normed, (((0,), (0,)), ((), ())), preferred_element_type=F32
        )
        packed[step] = rows_out.reshape(experts, cap, width).astype(BF16)
        leaving.append(
            pltpu.make_async_copy(packed.at[step], out_hbm.at[:, step], out_sem.at[step])
        )
        leaving[-1].start()
    for copy in leaving:
        copy.wait()


def weigh_kernel(routes_ref, gates_ref, out_ref):
    steps, top, rows = routes_ref.shape
    slots = out_ref.shape[2]
    owner = lax.broadcasted_iota(jnp.int32, (rows, slots), 1) >> 3
    for step in range(steps):
        named_by = routes_ref[step].T
        gate_of = gates_ref[step].T
        mask = slot_mask(named_by, slots // CAP)
        weight = jnp.zeros((rows, slots), F32)
        for k in range(top):
            weight = jnp.where(named_by[:, k : k + 1] == owner, gate_of[:, k : k + 1], weight)
        weight = jnp.where(mask, weight, 0.0)
        high = weight.astype(BF16)
        rest = weight - high.astype(F32)
        mid = rest.astype(BF16)
        low = (rest - mid.astype(F32)).astype(BF16)
        out_ref[step, 0:rows] = high
        out_ref[step, rows : 2 * rows] = mid
        out_ref[step, 2 * rows : 3 * rows] = low


def sort_kernel(core_ref, *refs):
    sources, (mine_ref, theirs_ref) = refs[:-2], refs[-2:]
    core = core_ref[0]
    shard = sources[0].shape[2]
    for i, source in enumerate(sources):
        place = pl.ds(i // 2 * shard, shard)
        mine_ref[i % 2, :, place] = source[core]
        theirs_ref[i % 2, :, place] = source[1 - core]


def join_kernel(*refs):
    parts, out_ref = refs[:-1], refs[-1]
    shard = parts[0].shape[2]
    for i, part in enumerate(parts):
        out_ref[:, :, i * shard : (i + 1) * shard] = part[...]


def expert_kernel(switch_ref, own_ref, rows_ref, *refs):
    blocks, (out_ref, weights, sem) = refs[:-3], refs[-3:]
    sources, steps, cap, width = rows_ref.shape
    mats, part = blocks[0].shape[1:3]
    first_new = switch_ref[own_ref[0]]
    version_at = lambda step: (step >= first_new).astype(jnp.int32)
    nt = (((1,), (1,)), ((), ()))

    def copies(version, i):
        return [
            pltpu.make_async_copy(
                block.at[version, i],
                weights.at[version, i, pl.ds(b * part, part)],
                sem.at[version, i, b],
            )
            for b, block in enumerate(blocks)
        ]

    def fetch(version):
        for i in range(mats):
            for copy in copies(version, i):
                copy.start()

    def arrive(version, i):
        for copy in copies(version, i):
            copy.wait()

    both = (first_new > 0) & (first_new < steps)
    fetch(version_at(0))
    pl.when(both)(lambda: fetch(1))
    for step in range(steps):
        version = version_at(step)
        if step == 0:
            arrive(version, 0)
        else:

            @pl.when(first_new == step)
            def _():
                for i in range(mats):
                    arrive(1, i)

        rows_in = rows_ref[:, step].astype(F32).reshape(sources * cap, width).astype(BF16)
        gate_v = lax.dot_general(rows_in, weights[version, 0], nt, preferred_element_type=F32)
        if step == 0:
            arrive(version, 1)
        up_v = lax.dot_general(rows_in, weights[version, 1], nt, preferred_element_type=F32)
        act = (gate_v / (1.0 + jnp.exp(-gate_v)) * up_v).astype(BF16)
        if step == 0:
            arrive(version, 2)
        made = jnp.dot(act, weights[version, 2], preferred_element_type=F32)
        out_ref[:, step] = made.reshape(sources, cap, width).astype(BF16)


def combine_kernel(hidden_ref, weights_ref, back_ref, out_ref):
    steps, rows, width = hidden_ref.shape
    experts, _, cap, _ = back_ref.shape
    for step in range(steps):
        outputs = back_ref[:, step].astype(F32).reshape(experts * cap, width).astype(BF16)
        parts = jnp.dot(weights_ref[step], outputs, preferred_element_type=F32)
        total = parts[2 * rows :] + parts[rows : 2 * rows] + parts[:rows]
        out_ref[step] = (hidden_ref[step].astype(F32) + total).astype(BF16)


def local(hidden, norm_gain, routes, gates, switch, experts_old, experts_new):
    steps, rows, width = hidden.shape
    top = routes.shape[2]
    exp_dev, mats, shard, _ = experts_old.shape
    members = lax.axis_size("expert")
    groups = lax.axis_size("group")
    experts = exp_dev * members
    slots = experts * CAP
    limit = lambda mib: pltpu.CompilerParams(vmem_limit_bytes=mib * 1024 * 1024)
    plane = groups // 2
    core = lax.axis_index("group") % 2

    def device(low, x, c):
        return (low % 2) * plane + (x % (plane // 2)) * 2 + c % 2

    def move(array, low, x, c):
        pairs = [
            (device(l, i, k), device(l + low, i + x, k + c))
            for l in range(2)
            for i in range(plane // 2)
            for k in range(2)
        ]
        return lax.ppermute(array, "group", pairs)

    bend = lambda e: (e + 1) % 4 // 2
    rings = [
        [device(low + bend(e), x, c) * members + e for e in range(members) for c in range(2)]
        for low in range(2)
        for x in range(plane // 2)
    ]

    def exchange(blocks):
        return lax.all_to_all(
            blocks, ("group", "expert"), 0, 0, axis_index_groups=rings, tiled=True
        )

    partner = [move(array, 1, 0, 0) for array in (experts_old, experts_new)]

    far = lambda array: pltpu.with_memory_space_constraint(array, pltpu.HBM)
    routes = routes.transpose(0, 2, 1)
    gates = gates.transpose(0, 2, 1)
    outgoing = pl.pallas_call(
        pack_kernel,
        in_specs=[pl.BlockSpec(memory_space=pltpu.HBM)] * 3,
        out_specs=pl.BlockSpec(memory_space=pltpu.HBM),
        out_shape=pltpu.HBM((experts, steps, CAP, width), BF16),
        scratch_shapes=[
            pltpu.VMEM(hidden.shape, BF16),
            pltpu.VMEM((1, width), F32),
            pltpu.VMEM((steps, top, rows), jnp.int32),
            pltpu.VMEM((steps, experts, CAP, width), BF16),
            pltpu.SemaphoreType.DMA((3,)),
            pltpu.SemaphoreType.DMA((steps,)),
        ],
        compiler_params=limit(16),
        cost_estimate=pl.CostEstimate(
            flops=2 * steps * rows * slots * width, bytes_accessed=4 << 20, transcendentals=0
        ),
        name="pack",
    )(far(hidden), far(norm_gain.reshape(1, width)), far(routes))
    weigh = pl.pallas_call(
        weigh_kernel,
        out_shape=jax.ShapeDtypeStruct((steps, 3 * rows, slots), BF16),
        compiler_params=limit(16),
        name="weigh",
    )(routes, gates)
    received = exchange(outgoing)
    near = (2, mats, 2 * shard, width)
    whole = pl.BlockSpec(memory_space=pltpu.VMEM)
    mine, theirs = pl.pallas_call(
        sort_kernel,
        in_specs=[pl.BlockSpec(memory_space=pltpu.SMEM)] + [whole] * 4,
        out_shape=(jax.ShapeDtypeStruct(near, BF16), jax.ShapeDtypeStruct(near, BF16)),
        compiler_params=limit(16),
        cost_estimate=pl.CostEstimate(flops=100_000_000_000, bytes_accessed=4 << 20, transcendentals=0),
        name="sort",
    )(core.reshape(1), experts_old, experts_new, *partner)
    block = pl.pallas_call(
        join_kernel,
        out_shape=jax.ShapeDtypeStruct((2, mats, 4 * shard, width), BF16),
        compiler_params=limit(16),
        name="join",
    )(mine, move(theirs, 0, 0, 1))
    blocks = [block] + [move(block, 0, x, 0) for x in (2, 1, -1)]

    received, weigh = lax.optimization_barrier((received, weigh))
    own = lax.axis_index("expert") * exp_dev + core
    produced = pl.pallas_call(
        expert_kernel,
        grid_spec=pltpu.PrefetchScalarGridSpec(
            num_scalar_prefetch=2,
            grid=(1,),
            in_specs=[whole] + [pl.BlockSpec(memory_space=pltpu.HBM)] * len(blocks),
            out_specs=whole,
            scratch_shapes=[
                pltpu.VMEM((2, mats, shard * groups, width), BF16),
                pltpu.SemaphoreType.DMA((2, mats, len(blocks))),
            ],
        ),
        out_shape=jax.ShapeDtypeStruct((experts, steps, CAP, width), BF16),
        compiler_params=limit(28),
        name="experts",
    )(switch, own.reshape(1), received, *(far(part) for part in blocks))
    returned = exchange(produced)
    return pl.pallas_call(
        combine_kernel,
        out_shape=jax.ShapeDtypeStruct((steps, rows, width), BF16),
        compiler_params=limit(16),
        name="combine",
    )(hidden, weigh, returned)


def solution(mesh):
    in_specs = (
        P(None, ("group", "expert"), None),
        P(),
        P(None, ("group", "expert"), None),
        P(None, ("group", "expert"), None),
        P(),
        P("expert", None, "group", None),
        P("expert", None, "group", None),
    )
    out_specs = P(None, ("group", "expert"), None)
    return jax.shard_map(local, mesh=mesh, in_specs=in_specs, out_specs=out_specs, check_vma=False)
```

```python
import jax
import jax.numpy as jnp
from jax import lax
from jax.experimental import pallas as pl
from jax.experimental.pallas import tpu as pltpu
from jax.sharding import PartitionSpec as P

CAP = 8
F32 = jnp.float32
BF16 = jnp.bfloat16


def slot_mask(routes, experts):
    rows, top = routes.shape
    slots = experts * CAP
    lane = lax.broadcasted_iota(jnp.int32, (rows, slots), 1)
    owner = lane >> 3
    named = routes[:, 0:1] == owner
    for k in range(1, top):
        named = named | (routes[:, k : k + 1] == owner)
    earlier = lax.broadcasted_iota(jnp.int32, (rows, rows), 1) < lax.broadcasted_iota(
        jnp.int32, (rows, rows), 0
    )
    rank = jnp.dot(
        earlier.astype(F32).astype(BF16), named.astype(F32).astype(BF16), preferred_element_type=F32
    )
    return named & (rank == (lane & 7).astype(F32))


def load_kernel(old_hbm, new_hbm, hidden_hbm, gain_hbm, routes_hbm, both, hidden, gain, routes, sem):
    moves = (
        (old_hbm, both.at[0]),
        (new_hbm, both.at[1]),
        (hidden_hbm, hidden),
        (gain_hbm, gain),
        (routes_hbm, routes),
    )
    copies = [
        pltpu.make_async_copy(source, held, sem.at[i]) for i, (source, held) in enumerate(moves)
    ]
    for copy in copies:
        copy.start()
    for copy in copies:
        copy.wait()


def pack_kernel(hidden, gain, routes, out_hbm, packed, sem):
    steps, experts, cap, width = packed.shape
    leaving = []
    for step in range(steps):
        xf = hidden[step].astype(F32)
        scale = lax.rsqrt(jnp.mean(xf * xf, axis=-1, keepdims=True) + 1e-06)
        normed = (xf * scale * gain[...]).astype(BF16)
        spread = slot_mask(routes[step].T, experts).astype(F32).astype(BF16)
        rows_out = lax.dot_general(
            spread, normed, (((0,), (0,)), ((), ())), preferred_element_type=F32
        )
        packed[step] = rows_out.reshape(experts, cap, width).astype(BF16)
        leaving.append(pltpu.make_async_copy(packed.at[step], out_hbm.at[:, step], sem.at[step]))
        leaving[-1].start()
    for copy in leaving:
        copy.wait()


def weigh_kernel(routes_ref, gates_ref, out_ref):
    steps, top, rows = routes_ref.shape
    slots = out_ref.shape[2]
    owner = lax.broadcasted_iota(jnp.int32, (rows, slots), 1) >> 3
    for step in range(steps):
        named_by = routes_ref[step].T
        gate_of = gates_ref[step].T
        mask = slot_mask(named_by, slots // CAP)
        weight = jnp.zeros((rows, slots), F32)
        for k in range(top):
            weight = jnp.where(named_by[:, k : k + 1] == owner, gate_of[:, k : k + 1], weight)
        weight = jnp.where(mask, weight, 0.0)
        high = weight.astype(BF16)
        rest = weight - high.astype(F32)
        mid = rest.astype(BF16)
        low = (rest - mid.astype(F32)).astype(BF16)
        out_ref[step, 0:rows] = high
        out_ref[step, rows : 2 * rows] = mid
        out_ref[step, 2 * rows : 3 * rows] = low


def sort_kernel(core_ref, *refs):
    sources, (mine_ref, theirs_ref) = refs[:-2], refs[-2:]
    core = core_ref[0]
    shard = sources[0].shape[3]
    for i, source in enumerate(sources):
        place = pl.ds(i * shard, shard)
        mine_ref[:, :, place] = source[:, core]
        theirs_ref[:, :, place] = source[:, 1 - core]


def join_kernel(*refs):
    parts, out_ref = refs[:-1], refs[-1]
    shard = parts[0].shape[2]
    for i, part in enumerate(parts):
        out_ref[:, :, i * shard : (i + 1) * shard] = part[...]


def stage_kernel(*refs):
    blocks, (out_ref, sem) = refs[:-2], refs[-2:]
    part = blocks[0].shape[2]
    copies = [
        pltpu.make_async_copy(block, out_ref.at[:, :, pl.ds(b * part, part)], sem.at[b])
        for b, block in enumerate(blocks)
    ]
    for copy in copies:
        copy.start()
    for copy in copies:
        copy.wait()


def expert_kernel(switch_ref, own_ref, rows_ref, weights_hbm, out_ref, weights, sem):
    sources, steps, cap, width = rows_ref.shape
    mats = weights.shape[1]
    first_new = switch_ref[own_ref[0]]
    version_at = lambda step: (step >= first_new).astype(jnp.int32)
    changes = (first_new > 0) & (first_new < steps)
    nt = (((1,), (1,)), ((), ()))

    def matrix(version, i):
        return pltpu.make_async_copy(
            weights_hbm.at[version, i], weights.at[version, i], sem.at[version, i]
        )

    for i in range(mats):
        matrix(version_at(0), i).start()

    @pl.when(changes)
    def _():
        for i in range(mats):
            matrix(1, i).start()

    for step in range(steps):
        version = version_at(step)
        rows_in = rows_ref[:, step].astype(F32).reshape(sources * cap, width).astype(BF16)
        if step == 0:
            matrix(version, 0).wait()
        gate_v = lax.dot_general(rows_in, weights[version, 0], nt, preferred_element_type=F32)
        if step == 0:
            matrix(version, 1).wait()
        up_v = lax.dot_general(rows_in, weights[version, 1], nt, preferred_element_type=F32)
        act = (gate_v / (1.0 + jnp.exp(-gate_v)) * up_v).astype(BF16)
        if step == 0:
            matrix(version, 2).wait()
        made = jnp.dot(act, weights[version, 2], preferred_element_type=F32)
        out_ref[:, step] = made.reshape(sources, cap, width).astype(BF16)
        if step == 0:

            @pl.when(changes)
            def _():
                for i in range(mats):
                    matrix(1, i).wait()


def combine_kernel(hidden_ref, weights_ref, back_ref, out_ref):
    steps, rows, width = hidden_ref.shape
    experts, _, cap, _ = back_ref.shape
    for step in range(steps):
        outputs = back_ref[:, step].astype(F32).reshape(experts * cap, width).astype(BF16)
        parts = jnp.dot(weights_ref[step], outputs, preferred_element_type=F32)
        total = parts[2 * rows :] + parts[rows : 2 * rows] + parts[:rows]
        out_ref[step] = (hidden_ref[step].astype(F32) + total).astype(BF16)


def local(hidden, norm_gain, routes, gates, switch, experts_old, experts_new):
    steps, rows, width = hidden.shape
    top = routes.shape[2]
    exp_dev, mats, shard, _ = experts_old.shape
    members = lax.axis_size("expert")
    groups = lax.axis_size("group")
    experts = exp_dev * members
    slots = experts * CAP
    limit = lambda mib: pltpu.CompilerParams(vmem_limit_bytes=mib * 1024 * 1024)
    plane = groups // 2
    core = lax.axis_index("group") % 2

    def device(low, x, c):
        return (low % 2) * plane + (x % (plane // 2)) * 2 + c % 2

    def move(array, low, x, c):
        pairs = [
            (device(l, i, k), device(l + low, i + x, k + c))
            for l in range(2)
            for i in range(plane // 2)
            for k in range(2)
        ]
        return lax.ppermute(array, "group", pairs)

    bend = lambda e: (e + 1) % 4 // 2
    rings = [
        [device(low + bend(e), x, c) * members + e for e in range(members) for c in range(2)]
        for low in range(2)
        for x in range(plane // 2)
    ]

    def exchange(blocks):
        return lax.all_to_all(
            blocks, ("group", "expert"), 0, 0, axis_index_groups=rings, tiled=True
        )

    far = lambda array: pltpu.with_memory_space_constraint(array, pltpu.HBM)
    routes = routes.transpose(0, 2, 1)
    gates = gates.transpose(0, 2, 1)
    whole = pl.BlockSpec(memory_space=pltpu.VMEM)
    inputs = (experts_old, experts_new, hidden, norm_gain.reshape(1, width), routes)
    both, *near_inputs = pl.pallas_call(
        load_kernel,
        in_specs=[pl.BlockSpec(memory_space=pltpu.HBM)] * len(inputs),
        out_specs=[whole] * (len(inputs) - 1),
        out_shape=[pltpu.VMEM((2,) + experts_old.shape, BF16)]
        + [pltpu.VMEM(array.shape, array.dtype) for array in inputs[2:]],
        scratch_shapes=[pltpu.SemaphoreType.DMA((len(inputs),))],
        compiler_params=limit(16),
        name="load",
    )(*(far(array) for array in inputs))
    outgoing = pl.pallas_call(
        pack_kernel,
        in_specs=[whole] * 3,
        out_specs=pl.BlockSpec(memory_space=pltpu.HBM),
        out_shape=pltpu.HBM((experts, steps, CAP, width), BF16),
        scratch_shapes=[
            pltpu.VMEM((steps, experts, CAP, width), BF16),
            pltpu.SemaphoreType.DMA((steps,)),
        ],
        compiler_params=limit(16),
        cost_estimate=pl.CostEstimate(
            flops=2 * steps * rows * slots * width, bytes_accessed=4 << 20, transcendentals=0
        ),
        name="pack",
    )(*near_inputs)
    weigh = pl.pallas_call(
        weigh_kernel,
        out_shape=jax.ShapeDtypeStruct((steps, 3 * rows, slots), BF16),
        compiler_params=limit(16),
        name="weigh",
    )(routes, gates)
    received = exchange(outgoing)
    near = (2, mats, 2 * shard, width)
    mine, theirs = pl.pallas_call(
        sort_kernel,
        in_specs=[pl.BlockSpec(memory_space=pltpu.SMEM)] + [whole] * 2,
        out_shape=(jax.ShapeDtypeStruct(near, BF16), jax.ShapeDtypeStruct(near, BF16)),
        compiler_params=limit(16),
        cost_estimate=pl.CostEstimate(flops=100_000_000_000, bytes_accessed=4 << 20, transcendentals=0),
        name="sort",
    )(core.reshape(1), both, move(both, 1, 0, 0))
    block = pl.pallas_call(
        join_kernel,
        out_shape=jax.ShapeDtypeStruct((2, mats, 4 * shard, width), BF16),
        compiler_params=limit(16),
        name="join",
    )(mine, move(theirs, 0, 0, 1))
    blocks = [block] + [move(block, 0, x, 0) for x in (2, 1, -1)]

    received, weigh = lax.optimization_barrier((received, weigh))
    staged = (2, mats, shard * groups, width)
    weights = pl.pallas_call(
        stage_kernel,
        in_specs=[pl.BlockSpec(memory_space=pltpu.HBM)] * len(blocks),
        out_specs=whole,
        out_shape=jax.ShapeDtypeStruct(staged, BF16),
        scratch_shapes=[pltpu.SemaphoreType.DMA((len(blocks),))],
        compiler_params=limit(16),
        cost_estimate=pl.CostEstimate(flops=10_000_000_000, bytes_accessed=9 << 20, transcendentals=0),
        name="stage",
    )(*(far(part) for part in blocks))
    own = lax.axis_index("expert") * exp_dev + core
    produced = pl.pallas_call(
        expert_kernel,
        grid_spec=pltpu.PrefetchScalarGridSpec(
            num_scalar_prefetch=2,
            grid=(1,),
            in_specs=[whole, pl.BlockSpec(memory_space=pltpu.HBM)],
            out_specs=whole,
            scratch_shapes=[pltpu.VMEM(staged, BF16), pltpu.SemaphoreType.DMA((2, mats))],
        ),
        out_shape=jax.ShapeDtypeStruct((experts, steps, CAP, width), BF16),
        compiler_params=limit(28),
        name="experts",
    )(switch, own.reshape(1), received, far(weights))
    returned = exchange(produced)
    return pl.pallas_call(
        combine_kernel,
        out_shape=jax.ShapeDtypeStruct((steps, rows, width), BF16),
        compiler_params=limit(16),
        name="combine",
    )(hidden, weigh, returned)


def solution(mesh):
    in_specs = (
        P(None, ("group", "expert"), None),
        P(),
        P(None, ("group", "expert"), None),
        P(None, ("group", "expert"), None),
        P(),
        P("expert", None, "group", None),
        P("expert", None, "group", None),
    )
    out_specs = P(None, ("group", "expert"), None)
    return jax.shard_map(local, mesh=mesh, in_specs=in_specs, out_specs=out_specs, check_vma=False)
```

```python
import jax
import jax.numpy as jnp
from jax import lax
from jax.experimental import pallas as pl
from jax.experimental.pallas import tpu as pltpu
from jax.sharding import PartitionSpec as P

CAP = 8
F32 = jnp.float32
BF16 = jnp.bfloat16


def slot_mask(routes, experts):
    rows, top = routes.shape
    slots = experts * CAP
    lane = lax.broadcasted_iota(jnp.int32, (rows, slots), 1)
    owner = lane >> 3
    named = routes[:, 0:1] == owner
    for k in range(1, top):
        named = named | (routes[:, k : k + 1] == owner)
    earlier = lax.broadcasted_iota(jnp.int32, (rows, rows), 1) < lax.broadcasted_iota(
        jnp.int32, (rows, rows), 0
    )
    rank = jnp.dot(
        earlier.astype(F32).astype(BF16), named.astype(F32).astype(BF16), preferred_element_type=F32
    )
    return named & (rank == (lane & 7).astype(F32))


def load_kernel(old_hbm, new_hbm, hidden_hbm, gain_hbm, routes_hbm, both, hidden, gain, routes, sem):
    moves = (
        (old_hbm, both.at[0]),
        (new_hbm, both.at[1]),
        (hidden_hbm, hidden),
        (gain_hbm, gain),
        (routes_hbm, routes),
    )
    copies = [
        pltpu.make_async_copy(source, held, sem.at[i]) for i, (source, held) in enumerate(moves)
    ]
    for copy in copies:
        copy.start()
    for copy in copies:
        copy.wait()


def pack_kernel(hidden, gain, routes, out_hbm, packed, sem):
    steps, experts, cap, width = packed.shape
    leaving = []
    for step in range(steps):
        xf = hidden[step].astype(F32)
        scale = lax.rsqrt(jnp.mean(xf * xf, axis=-1, keepdims=True) + 1e-06)
        normed = (xf * scale * gain[...]).astype(BF16)
        spread = slot_mask(routes[step].T, experts).astype(F32).astype(BF16)
        rows_out = lax.dot_general(
            spread, normed, (((0,), (0,)), ((), ())), preferred_element_type=F32
        )
        packed[step] = rows_out.reshape(experts, cap, width).astype(BF16)
        leaving.append(pltpu.make_async_copy(packed.at[step], out_hbm.at[:, step], sem.at[step]))
        leaving[-1].start()
    for copy in leaving:
        copy.wait()


def weigh_kernel(routes_ref, gates_ref, out_ref):
    steps, top, rows = routes_ref.shape
    slots = out_ref.shape[2]
    owner = lax.broadcasted_iota(jnp.int32, (rows, slots), 1) >> 3
    for step in range(steps):
        named_by = routes_ref[step].T
        gate_of = gates_ref[step].T
        mask = slot_mask(named_by, slots // CAP)
        weight = jnp.zeros((rows, slots), F32)
        for k in range(top):
            weight = jnp.where(named_by[:, k : k + 1] == owner, gate_of[:, k : k + 1], weight)
        weight = jnp.where(mask, weight, 0.0)
        high = weight.astype(BF16)
        rest = weight - high.astype(F32)
        mid = rest.astype(BF16)
        low = (rest - mid.astype(F32)).astype(BF16)
        out_ref[step, 0:rows] = high
        out_ref[step, rows : 2 * rows] = mid
        out_ref[step, 2 * rows : 3 * rows] = low


def sort_kernel(core_ref, *refs):
    sources, (mine_ref, theirs_ref) = refs[:-2], refs[-2:]
    core = core_ref[0]
    shard = sources[0].shape[3]
    for i, source in enumerate(sources):
        place = pl.ds(i * shard, shard)
        mine_ref[:, :, place] = source[:, core]
        theirs_ref[:, :, place] = source[:, 1 - core]


def join_kernel(*refs):
    parts, out_ref = refs[:-1], refs[-1]
    shard = parts[0].shape[2]
    for i, part in enumerate(parts):
        out_ref[:, :, i * shard : (i + 1) * shard] = part[...]


def stage_kernel(*refs):
    blocks, (out_ref, sem) = refs[:-2], refs[-2:]
    part = blocks[0].shape[2]
    copies = [
        pltpu.make_async_copy(block, out_ref.at[:, :, pl.ds(b * part, part)], sem.at[b])
        for b, block in enumerate(blocks)
    ]
    for copy in copies:
        copy.start()
    for copy in copies:
        copy.wait()


def expert_kernel(switch_ref, own_ref, rows_ref, weights_hbm, out_ref, weights, sem):
    sources, steps, cap, width = rows_ref.shape
    mats = weights.shape[1]
    first_new = switch_ref[own_ref[0]]
    version_at = lambda step: (step >= first_new).astype(jnp.int32)
    changes = (first_new > 0) & (first_new < steps)
    nt = (((1,), (1,)), ((), ()))

    def matrix(version, i):
        return pltpu.make_async_copy(
            weights_hbm.at[version, i], weights.at[version, i], sem.at[version, i]
        )

    for i in range(mats):
        matrix(version_at(0), i).start()

    @pl.when(changes)
    def _():
        for i in range(mats):
            matrix(1, i).start()

    for step in range(steps):
        version = version_at(step)
        rows_in = rows_ref[:, step].astype(F32).reshape(sources * cap, width).astype(BF16)
        if step == 0:
            matrix(version, 0).wait()
        gate_v = lax.dot_general(rows_in, weights[version, 0], nt, preferred_element_type=F32)
        if step == 0:
            matrix(version, 1).wait()
        up_v = lax.dot_general(rows_in, weights[version, 1], nt, preferred_element_type=F32)
        act = (gate_v / (1.0 + jnp.exp(-gate_v)) * up_v).astype(BF16)
        if step == 0:
            matrix(version, 2).wait()
        made = jnp.dot(act, weights[version, 2], preferred_element_type=F32)
        out_ref[:, step] = made.reshape(sources, cap, width).astype(BF16)
        if step == 0:

            @pl.when(changes)
            def _():
                for i in range(mats):
                    matrix(1, i).wait()


def combine_kernel(hidden_ref, weights_ref, back_ref, out_ref):
    steps, rows, width = hidden_ref.shape
    experts, _, cap, _ = back_ref.shape
    for step in range(steps):
        outputs = back_ref[:, step].astype(F32).reshape(experts * cap, width).astype(BF16)
        parts = jnp.dot(weights_ref[step], outputs, preferred_element_type=F32)
        total = parts[2 * rows :] + parts[rows : 2 * rows] + parts[:rows]
        out_ref[step] = (hidden_ref[step].astype(F32) + total).astype(BF16)


def local(hidden, norm_gain, routes, gates, switch, experts_old, experts_new):
    steps, rows, width = hidden.shape
    top = routes.shape[2]
    exp_dev, mats, shard, _ = experts_old.shape
    members = lax.axis_size("expert")
    groups = lax.axis_size("group")
    experts = exp_dev * members
    slots = experts * CAP
    limit = lambda mib: pltpu.CompilerParams(vmem_limit_bytes=mib * 1024 * 1024)
    plane = groups // 2
    core = lax.axis_index("group") % 2

    def device(low, x, c):
        return (low % 2) * plane + (x % (plane // 2)) * 2 + c % 2

    def move(array, low, x, c):
        pairs = [
            (device(l, i, k), device(l + low, i + x, k + c))
            for l in range(2)
            for i in range(plane // 2)
            for k in range(2)
        ]
        return lax.ppermute(array, "group", pairs)

    bend = lambda e: e % 4 // 2
    rings = [
        [device(low + bend(e), x, c) * members + e for e in range(members) for c in range(2)]
        for low in range(2)
        for x in range(plane // 2)
    ]

    def exchange(blocks):
        return lax.all_to_all(
            blocks, ("group", "expert"), 0, 0, axis_index_groups=rings, tiled=True
        )

    far = lambda array: pltpu.with_memory_space_constraint(array, pltpu.HBM)
    routes = routes.transpose(0, 2, 1)
    gates = gates.transpose(0, 2, 1)
    whole = pl.BlockSpec(memory_space=pltpu.VMEM)
    inputs = (experts_old, experts_new, hidden, norm_gain.reshape(1, width), routes)
    both, *near_inputs = pl.pallas_call(
        load_kernel,
        in_specs=[pl.BlockSpec(memory_space=pltpu.HBM)] * len(inputs),
        out_specs=[whole] * (len(inputs) - 1),
        out_shape=[pltpu.VMEM((2,) + experts_old.shape, BF16)]
        + [pltpu.VMEM(array.shape, array.dtype) for array in inputs[2:]],
        scratch_shapes=[pltpu.SemaphoreType.DMA((len(inputs),))],
        compiler_params=limit(16),
        name="load",
    )(*(far(array) for array in inputs))
    outgoing = pl.pallas_call(
        pack_kernel,
        in_specs=[whole] * 3,
        out_specs=pl.BlockSpec(memory_space=pltpu.HBM),
        out_shape=pltpu.HBM((experts, steps, CAP, width), BF16),
        scratch_shapes=[
            pltpu.VMEM((steps, experts, CAP, width), BF16),
            pltpu.SemaphoreType.DMA((steps,)),
        ],
        compiler_params=limit(16),
        cost_estimate=pl.CostEstimate(
            flops=2 * steps * rows * slots * width, bytes_accessed=4 << 20, transcendentals=0
        ),
        name="pack",
    )(*near_inputs)
    weigh = pl.pallas_call(
        weigh_kernel,
        out_shape=jax.ShapeDtypeStruct((steps, 3 * rows, slots), BF16),
        compiler_params=limit(16),
        name="weigh",
    )(routes, gates)
    received = exchange(outgoing)
    near = (2, mats, 2 * shard, width)
    mine, theirs = pl.pallas_call(
        sort_kernel,
        in_specs=[pl.BlockSpec(memory_space=pltpu.SMEM)] + [whole] * 2,
        out_shape=(jax.ShapeDtypeStruct(near, BF16), jax.ShapeDtypeStruct(near, BF16)),
        compiler_params=limit(16),
        cost_estimate=pl.CostEstimate(flops=100_000_000_000, bytes_accessed=4 << 20, transcendentals=0),
        name="sort",
    )(core.reshape(1), both, move(both, 1, 0, 0))
    block = pl.pallas_call(
        join_kernel,
        out_shape=jax.ShapeDtypeStruct((2, mats, 4 * shard, width), BF16),
        compiler_params=limit(16),
        name="join",
    )(mine, move(theirs, 0, 0, 1))
    blocks = [block] + [move(block, 0, x, 0) for x in (2, 1, -1)]

    received, weigh = lax.optimization_barrier((received, weigh))
    staged = (2, mats, shard * groups, width)
    weights = pl.pallas_call(
        stage_kernel,
        in_specs=[pl.BlockSpec(memory_space=pltpu.HBM)] * len(blocks),
        out_specs=whole,
        out_shape=jax.ShapeDtypeStruct(staged, BF16),
        scratch_shapes=[pltpu.SemaphoreType.DMA((len(blocks),))],
        compiler_params=limit(16),
        cost_estimate=pl.CostEstimate(flops=10_000_000_000, bytes_accessed=9 << 20, transcendentals=0),
        name="stage",
    )(*(far(part) for part in blocks))
    own = lax.axis_index("expert") * exp_dev + core
    produced = pl.pallas_call(
        expert_kernel,
        grid_spec=pltpu.PrefetchScalarGridSpec(
            num_scalar_prefetch=2,
            grid=(1,),
            in_specs=[whole, pl.BlockSpec(memory_space=pltpu.HBM)],
            out_specs=whole,
            scratch_shapes=[pltpu.VMEM(staged, BF16), pltpu.SemaphoreType.DMA((2, mats))],
        ),
        out_shape=jax.ShapeDtypeStruct((experts, steps, CAP, width), BF16),
        compiler_params=limit(28),
        name="experts",
    )(switch, own.reshape(1), received, far(weights))
    returned = exchange(produced)
    return pl.pallas_call(
        combine_kernel,
        out_shape=jax.ShapeDtypeStruct((steps, rows, width), BF16),
        compiler_params=limit(16),
        name="combine",
    )(hidden, weigh, returned)


def solution(mesh):
    in_specs = (
        P(None, ("group", "expert"), None),
        P(),
        P(None, ("group", "expert"), None),
        P(None, ("group", "expert"), None),
        P(),
        P("expert", None, "group", None),
        P("expert", None, "group", None),
    )
    out_specs = P(None, ("group", "expert"), None)
    return jax.shard_map(local, mesh=mesh, in_specs=in_specs, out_specs=out_specs, check_vma=False)
```

```python
import jax
import jax.numpy as jnp
from jax import lax
from jax.experimental import pallas as pl
from jax.experimental.pallas import tpu as pltpu
from jax.sharding import PartitionSpec as P

CAP = 8
F32 = jnp.float32
BF16 = jnp.bfloat16


def slot_mask(routes, experts):
    rows, top = routes.shape
    slots = experts * CAP
    lane = lax.broadcasted_iota(jnp.int32, (rows, slots), 1)
    owner = lane >> 3
    named = routes[:, 0:1] == owner
    for k in range(1, top):
        named = named | (routes[:, k : k + 1] == owner)
    earlier = lax.broadcasted_iota(jnp.int32, (rows, rows), 1) < lax.broadcasted_iota(
        jnp.int32, (rows, rows), 0
    )
    rank = jnp.dot(
        earlier.astype(F32).astype(BF16), named.astype(F32).astype(BF16), preferred_element_type=F32
    )
    return named & (rank == (lane & 7).astype(F32))


def load_kernel(
    old_hbm, new_hbm, hidden_hbm, gain_hbm, routes_hbm, both_hbm, hidden, gain, routes, both, sem, out_sem
):
    moves = (
        (old_hbm, both.at[0]),
        (new_hbm, both.at[1]),
        (hidden_hbm, hidden),
        (gain_hbm, gain),
        (routes_hbm, routes),
    )
    copies = [
        pltpu.make_async_copy(source, held, sem.at[i]) for i, (source, held) in enumerate(moves)
    ]
    for copy in copies:
        copy.start()
    leaving = [
        pltpu.make_async_copy(both.at[i], both_hbm.at[i], out_sem.at[i]) for i in range(2)
    ]
    for i in range(2):
        copies[i].wait()
        leaving[i].start()
    for copy in copies[2:]:
        copy.wait()
    for copy in leaving:
        copy.wait()


def pack_kernel(hidden, gain, routes, out_hbm, packed, sem):
    steps, experts, cap, width = packed.shape
    leaving = []
    for step in range(steps):
        xf = hidden[step].astype(F32)
        scale = lax.rsqrt(jnp.mean(xf * xf, axis=-1, keepdims=True) + 1e-06)
        normed = (xf * scale * gain[...]).astype(BF16)
        spread = slot_mask(routes[step].T, experts).astype(F32).astype(BF16)
        half = experts // 2
        for i in range(2):
            rows_out = lax.dot_general(
                spread[:, i * half * cap : (i + 1) * half * cap],
                normed,
                (((0,), (0,)), ((), ())),
                preferred_element_type=F32,
            )
            place = pl.ds(i * half, half)
            packed[step, place] = rows_out.reshape(half, cap, width).astype(BF16)
            leaving.append(
                pltpu.make_async_copy(
                    packed.at[step, place], out_hbm.at[place, step], sem.at[step, i]
                )
            )
            leaving[-1].start()
    for copy in leaving:
        copy.wait()


def weigh_kernel(routes_ref, gates_ref, out_ref):
    steps, top, rows = routes_ref.shape
    slots = out_ref.shape[2]
    owner = lax.broadcasted_iota(jnp.int32, (rows, slots), 1) >> 3
    for step in range(steps):
        named_by = routes_ref[step].T
        gate_of = gates_ref[step].T
        mask = slot_mask(named_by, slots // CAP)
        weight = jnp.zeros((rows, slots), F32)
        for k in range(top):
            weight = jnp.where(named_by[:, k : k + 1] == owner, gate_of[:, k : k + 1], weight)
        weight = jnp.where(mask, weight, 0.0)
        high = weight.astype(BF16)
        rest = weight - high.astype(F32)
        mid = rest.astype(BF16)
        low = (rest - mid.astype(F32)).astype(BF16)
        out_ref[step, 0:rows] = high
        out_ref[step, rows : 2 * rows] = mid
        out_ref[step, 2 * rows : 3 * rows] = low


def sort_kernel(core_ref, *refs):
    sources, (mine_ref, theirs_ref) = refs[:-2], refs[-2:]
    core = core_ref[0]
    shard = sources[0].shape[3]
    for i, source in enumerate(sources):
        place = pl.ds(i * shard, shard)
        mine_ref[:, :, place] = source[:, core]
        theirs_ref[:, :, place] = source[:, 1 - core]


def join_kernel(*refs):
    parts, out_ref = refs[:-1], refs[-1]
    shard = parts[0].shape[2]
    for i, part in enumerate(parts):
        out_ref[:, :, i * shard : (i + 1) * shard] = part[...]


def stage_kernel(*refs):
    blocks, (out_ref, sem) = refs[:-2], refs[-2:]
    part = blocks[0].shape[2]
    copies = [
        pltpu.make_async_copy(block, out_ref.at[:, :, pl.ds(b * part, part)], sem.at[b])
        for b, block in enumerate(blocks)
    ]
    for copy in copies:
        copy.start()
    for copy in copies:
        copy.wait()


def expert_kernel(switch_ref, own_ref, rows_ref, weights_hbm, out_ref, weights, sem):
    sources, steps, cap, width = rows_ref.shape
    mats = weights.shape[1]
    first_new = switch_ref[own_ref[0]]
    version_at = lambda step: (step >= first_new).astype(jnp.int32)
    changes = (first_new > 0) & (first_new < steps)
    nt = (((1,), (1,)), ((), ()))

    def matrix(version, i):
        return pltpu.make_async_copy(
            weights_hbm.at[version, i], weights.at[version, i], sem.at[version, i]
        )

    for i in range(mats):
        matrix(version_at(0), i).start()

    @pl.when(changes)
    def _():
        for i in range(mats):
            matrix(1, i).start()

    for step in range(steps):
        version = version_at(step)
        rows_in = rows_ref[:, step].astype(F32).reshape(sources * cap, width).astype(BF16)
        if step == 0:
            matrix(version, 0).wait()
        gate_v = lax.dot_general(rows_in, weights[version, 0], nt, preferred_element_type=F32)
        if step == 0:
            matrix(version, 1).wait()
        up_v = lax.dot_general(rows_in, weights[version, 1], nt, preferred_element_type=F32)
        act = (gate_v / (1.0 + jnp.exp(-gate_v)) * up_v).astype(BF16)
        if step == 0:
            matrix(version, 2).wait()

            @pl.when(changes)
            def _():
                for i in range(mats):
                    matrix(1, i).wait()

        made = jnp.dot(act, weights[version, 2], preferred_element_type=F32)
        out_ref[:, step] = made.reshape(sources, cap, width).astype(BF16)

def combine_kernel(hidden_ref, weights_ref, back_ref, out_ref):
    steps, rows, width = hidden_ref.shape
    experts, _, cap, _ = back_ref.shape
    for step in range(steps):
        outputs = back_ref[:, step].astype(F32).reshape(experts * cap, width).astype(BF16)
        parts = jnp.dot(weights_ref[step], outputs, preferred_element_type=F32)
        total = parts[2 * rows :] + parts[rows : 2 * rows] + parts[:rows]
        out_ref[step] = (hidden_ref[step].astype(F32) + total).astype(BF16)


def local(hidden, norm_gain, routes, gates, switch, experts_old, experts_new):
    steps, rows, width = hidden.shape
    top = routes.shape[2]
    exp_dev, mats, shard, _ = experts_old.shape
    members = lax.axis_size("expert")
    groups = lax.axis_size("group")
    experts = exp_dev * members
    slots = experts * CAP
    limit = lambda mib: pltpu.CompilerParams(vmem_limit_bytes=mib * 1024 * 1024)
    plane = groups // 2
    core = lax.axis_index("group") % 2

    def device(low, x, c):
        return (low % 2) * plane + (x % (plane // 2)) * 2 + c % 2

    def move(array, low, x, c):
        pairs = [
            (device(l, i, k), device(l + low, i + x, k + c))
            for l in range(2)
            for i in range(plane // 2)
            for k in range(2)
        ]
        return lax.ppermute(array, "group", pairs)

    bend = lambda e: e % 4 // 2
    rings = [
        [device(low + bend(e), x, c) * members + e for e in range(members) for c in range(2)]
        for low in range(2)
        for x in range(plane // 2)
    ]

    def exchange(blocks):
        return lax.all_to_all(
            blocks, ("group", "expert"), 0, 0, axis_index_groups=rings, tiled=True
        )

    far = lambda array: pltpu.with_memory_space_constraint(array, pltpu.HBM)
    routes = routes.transpose(0, 2, 1)
    gates = gates.transpose(0, 2, 1)
    whole = pl.BlockSpec(memory_space=pltpu.VMEM)
    inputs = (experts_old, experts_new, hidden, norm_gain.reshape(1, width), routes)
    both, *near_inputs = pl.pallas_call(
        load_kernel,
        in_specs=[pl.BlockSpec(memory_space=pltpu.HBM)] * len(inputs),
        out_specs=[pl.BlockSpec(memory_space=pltpu.HBM)] + [whole] * (len(inputs) - 2),
        out_shape=[pltpu.HBM((2,) + experts_old.shape, BF16)]
        + [pltpu.VMEM(array.shape, array.dtype) for array in inputs[2:]],
        scratch_shapes=[
            pltpu.VMEM((2,) + experts_old.shape, BF16),
            pltpu.SemaphoreType.DMA((len(inputs),)),
            pltpu.SemaphoreType.DMA((2,)),
        ],
        compiler_params=limit(16),
        name="load",
    )(*(far(array) for array in inputs))
    outgoing = pl.pallas_call(
        pack_kernel,
        in_specs=[whole] * 3,
        out_specs=pl.BlockSpec(memory_space=pltpu.HBM),
        out_shape=pltpu.HBM((experts, steps, CAP, width), BF16),
        scratch_shapes=[
            pltpu.VMEM((steps, experts, CAP, width), BF16),
            pltpu.SemaphoreType.DMA((steps, 2)),
        ],
        compiler_params=limit(16),
        cost_estimate=pl.CostEstimate(
            flops=2 * steps * rows * slots * width, bytes_accessed=4 << 20, transcendentals=0
        ),
        name="pack",
    )(*near_inputs)
    weigh = pl.pallas_call(
        weigh_kernel,
        out_shape=jax.ShapeDtypeStruct((steps, 3 * rows, slots), BF16),
        compiler_params=limit(16),
        name="weigh",
    )(routes, gates)
    received = exchange(outgoing)
    near = (2, mats, 2 * shard, width)
    mine, theirs = pl.pallas_call(
        sort_kernel,
        in_specs=[pl.BlockSpec(memory_space=pltpu.SMEM)] + [whole] * 2,
        out_shape=(jax.ShapeDtypeStruct(near, BF16), jax.ShapeDtypeStruct(near, BF16)),
        compiler_params=limit(16),
        cost_estimate=pl.CostEstimate(flops=100_000_000_000, bytes_accessed=4 << 20, transcendentals=0),
        name="sort",
    )(core.reshape(1), both, move(both, 1, 0, 0))
    block = pl.pallas_call(
        join_kernel,
        out_shape=jax.ShapeDtypeStruct((2, mats, 4 * shard, width), BF16),
        compiler_params=limit(16),
        name="join",
    )(mine, move(theirs, 0, 0, 1))
    blocks = [block] + [move(block, 0, x, 0) for x in (2, 1, -1)]

    received, weigh = lax.optimization_barrier((received, weigh))
    staged = (2, mats, shard * groups, width)
    weights = pl.pallas_call(
        stage_kernel,
        in_specs=[pl.BlockSpec(memory_space=pltpu.HBM)] * len(blocks),
        out_specs=whole,
        out_shape=jax.ShapeDtypeStruct(staged, BF16),
        scratch_shapes=[pltpu.SemaphoreType.DMA((len(blocks),))],
        compiler_params=limit(16),
        cost_estimate=pl.CostEstimate(flops=10_000_000_000, bytes_accessed=9 << 20, transcendentals=0),
        name="stage",
    )(*(far(part) for part in blocks))
    own = lax.axis_index("expert") * exp_dev + core
    produced = pl.pallas_call(
        expert_kernel,
        grid_spec=pltpu.PrefetchScalarGridSpec(
            num_scalar_prefetch=2,
            grid=(1,),
            in_specs=[whole, pl.BlockSpec(memory_space=pltpu.HBM)],
            out_specs=whole,
            scratch_shapes=[pltpu.VMEM(staged, BF16), pltpu.SemaphoreType.DMA((2, mats))],
        ),
        out_shape=jax.ShapeDtypeStruct((experts, steps, CAP, width), BF16),
        compiler_params=limit(28),
        name="experts",
    )(switch, own.reshape(1), received, far(weights))
    returned = exchange(produced)
    return pl.pallas_call(
        combine_kernel,
        out_shape=jax.ShapeDtypeStruct((steps, rows, width), BF16),
        compiler_params=limit(16),
        name="combine",
    )(hidden, weigh, returned)


def solution(mesh):
    in_specs = (
        P(None, ("group", "expert"), None),
        P(),
        P(None, ("group", "expert"), None),
        P(None, ("group", "expert"), None),
        P(),
        P("expert", None, "group", None),
        P("expert", None, "group", None),
    )
    out_specs = P(None, ("group", "expert"), None)
    return jax.shard_map(local, mesh=mesh, in_specs=in_specs, out_specs=out_specs, check_vma=False)
```
